256 devices in a mesh: replica: 16 (over x, z_hi), shard: 16 (over y, z_lo, core).
Axes of the slice: x: 4, y: 4, z: 8 (z_hi: 4, z_lo: 2; z = z_hi * 2 + z_lo), core: 2. Of those that a mesh axis runs over, the one named last changes fastest.
Arguments:
- params: float32 [16, 4096, 512], P('replica', 'shard'), may hold values from -0.09375 to 0.09375
- moment: float32 [16, 4096, 512], P('replica', 'shard'), may hold values from -0.06 to 0.06
- inputs: bfloat16 [16, 8192, 4096], P('replica', 'shard'), may hold values from -6 to 6
- targets: bfloat16 [16, 8192, 512], P('replica', 'shard'), may hold values from -6 to 6
- step: int32 [1], replicated, may hold values from 0 to 63
Outputs:
- new_params: float32 [16, 4096, 512], P('replica', 'shard')
- new_moment: float32 [16, 4096, 512], P('replica', 'shard')
The draws below stay inside these ranges and needn't reach their ends.
All inputs are finite; a program needn't handle non-finite values.
Results may differ from the reference program's by a relative error of at most 0.0035.
Values may be sent and summed in bfloat16 or wider, within the bound.
No kernel may reach another device: no remote copies, remote signals or barrier semaphores. Data moves between devices by JAX's collectives and lax.ppermute only.
A program may use at most 64 MiB of HBM per device.

```python
import jax
import jax.numpy as jnp
from jax import lax

D = 4096
KV = 512
TOKENS = 8192
REPLICAS = 16


def block_scale(stream_key, dims, split, smallest, high):
    loudness = 1.0
    for dim, shards_of in split:
        steps = jax.random.uniform(jax.random.fold_in(jax.random.fold_in(stream_key, 6), dim), (shards_of,), jnp.float32, smallest / len(split), high / len(split))
        loudness = loudness * jnp.repeat(jnp.exp(steps), dims[dim] // shards_of).reshape((-1,) + (1,) * (len(dims) - 1 - dim))
    return loudness


def normal_values(stream_key, extent, scale, reach, split=(), held_as=jnp.bfloat16):
    result = jax.random.normal(stream_key, extent, jnp.float32) * scale
    if len(split) > 0:
        result = block_scale(stream_key, extent, split, -0.22, 0.18) * result
    return jnp.clip(result, min=-reach, max=reach).astype(held_as)


def setup_inputs(seed: int = 0) -> dict:
    streams_of = jax.random.split(jax.random.key(seed), 6)
    params = normal_values(streams_of[0], (REPLICAS, D, KV), D ** -0.5, 0.09375, ((0, 16), (1, 16)), jnp.float32)
    moment = normal_values(streams_of[1], (REPLICAS, D, KV), 0.01, 0.06, ((0, 16), (1, 16)), jnp.float32)
    inputs = normal_values(streams_of[2], (REPLICAS, TOKENS, D), 1.0, 6.0, ((0, 16), (1, 16)))
    targets = normal_values(streams_of[3], (REPLICAS, TOKENS, KV), 1.0, 6.0, ((0, 16), (1, 16)))
    step = jax.random.randint(streams_of[4], (1,), 0, 64).astype(jnp.int32)
    return {"params": params, "moment": moment, "inputs": inputs, "targets": targets, "step": step}


def replica_grad(args):
    weights, inputs, targets = args
    low = weights.astype(jnp.bfloat16)
    pred = jnp.dot(inputs, low, preferred_element_type=jnp.float32)
    resid = (pred - targets.astype(jnp.float32)).astype(jnp.bfloat16)
    grad = jnp.dot(inputs.T, resid, preferred_element_type=jnp.float32)
    return grad / jnp.float32(TOKENS)

def reference(params, moment, inputs, targets, step):
    weights = params
    momentum = moment
    for offset in range(2):
        now = step[0] + offset
        grad = lax.map(replica_grad, (weights, inputs, targets))
        upd_moment = 0.9 * momentum + grad
        upd_params = weights - 0.5 * upd_moment
        distance = (2 ** (now % 4)).astype(jnp.int32)
        weights = 0.5 * (upd_params + jnp.roll(upd_params, -distance, axis=0))
        momentum = 0.5 * (upd_moment + jnp.roll(upd_moment, -distance, axis=0))
    return (weights, momentum)
```

```python
from functools import partial

import jax
import jax.numpy as jnp
from jax import lax
from jax.sharding import PartitionSpec as P

BF16 = jnp.bfloat16
F32 = jnp.float32

CORE = [(i, i ^ 1) for i in range(16)]
ACROSS = [(i, i ^ 2) for i in range(16)]
UP = [(i, (i + 4) % 16) for i in range(16)]
DOWN = [(i, (i - 4) % 16) for i in range(16)]
FAR = [(i, (i + 8) % 16) for i in range(16)]


def move(value, route):
    return lax.ppermute(value, "shard", route)


def from_peer(value, distance):
    size = lax.axis_size("replica")
    return lax.ppermute(value, "replica", [((i + distance) % size, i) for i in range(size)])


def dot(a, b, over_a, over_b):
    return lax.dot_general(a, b, (((over_a,), (over_b,)), ((), ())), preferred_element_type=F32)


def halves(value, axis, core):
    low, high = jnp.split(value, 2, axis)
    first = core == 0
    return jnp.where(first, low, high), jnp.where(first, high, low)


def joined(kept, got, axis, core):
    first = core == 0
    return jnp.concatenate([jnp.where(first, kept, got), jnp.where(first, got, kept)], axis)


def to_columns(value, core):
    kept, sent = halves(value, 1, core)
    return joined(kept, move(sent, CORE), 0, core)


def to_rows(value, core):
    kept, sent = halves(value, 0, core)
    return joined(kept, move(sent, CORE), 1, core)


def gathered(block):
    across = move(block, ACROSS)
    below = move(block, UP)
    above = move(block, DOWN)
    far = move(block, FAR)
    return {
        (0, 0): block,
        (3, 0): below,
        (1, 0): above,
        (2, 0): far,
        (0, 1): across,
        (3, 1): move(across, UP),
        (1, 1): move(across, DOWN),
        (2, 1): move(far, ACROSS),
    }


def summed(part):
    low = lambda value: value.astype(BF16)
    wide = lambda value: value.astype(F32)
    to_below = move(low(part(3, 1)), DOWN)
    to_above = move(low(part(1, 1)), UP)
    to_far = move(low(part(2, 1)), ACROSS)
    below = move(low(part(3, 0)), DOWN)
    above = move(low(part(1, 0)), UP)
    far = move(low(part(2, 0) + wide(to_far)), FAR)
    across = move(low(part(0, 1) + wide(to_below) + wide(to_above)), ACROSS)
    return part(0, 0) + wide(below) + wide(above) + wide(far) + wide(across)


def local_grad(weights, blocks, targets, tokens_all):
    pred = jnp.zeros(targets.shape, F32)
    for place, low in gathered(weights.astype(BF16)).items():
        pred = pred + dot(blocks[place], low, 1, 0)
    resid = (pred - targets.astype(F32)).astype(BF16)
    total = summed(lambda dy, dz: dot(blocks[dy, dz], resid, 0, 0))
    return total / jnp.float32(tokens_all)


def two_steps(params, moment, inputs, targets, first):
    place = lax.axis_index("shard")
    core, z, y = place % 2, (place // 2) % 2, place // 4
    tokens_all = inputs.shape[0] * lax.axis_size("shard")

    weights = to_columns(params, core)
    momentum = to_columns(moment, core)
    kept, sent = halves(targets, 1, core)
    targets = jnp.concatenate([kept, move(sent, CORE)], 0)
    tokens = jnp.concatenate([inputs, move(inputs, CORE)], 0)
    width = weights.shape[0]
    blocks = {}
    for dy in range(4):
        for dz in range(2):
            chip = ((y + dy) % 4) * 2 + (z + dz) % 2
            blocks[dy, dz] = lax.dynamic_slice_in_dim(tokens, chip * width, width, 1)

    distance = 2 ** (first % 4)
    grad = local_grad(weights, blocks, targets, tokens_all)
    upd_moment = 0.9 * momentum + grad
    upd_params = weights - 0.5 * upd_moment
    weights = 0.5 * (upd_params + from_peer(upd_params.astype(BF16), distance).astype(F32))
    momentum = 0.5 * (upd_moment + from_peer(upd_moment.astype(BF16), distance).astype(F32))

    distance = 2 ** ((first + 1) % 4)
    decayed = 0.9 * momentum
    moved = weights - 0.5 * decayed
    peer_decayed = from_peer(decayed.astype(BF16), distance).astype(F32)
    peer_moved = from_peer(moved.astype(BF16), distance).astype(F32)
    grad = local_grad(weights, blocks, targets, tokens_all)
    both = grad + from_peer(grad.astype(BF16), distance).astype(F32)
    weights = 0.5 * (moved + peer_moved - 0.5 * both)
    momentum = 0.5 * (decayed + peer_decayed + both)
    return to_rows(weights, core)[None], to_rows(momentum, core)[None]


def local(params, moment, inputs, targets, step):
    branches = [partial(two_steps, first=first) for first in range(4)]
    return lax.switch(step[0] % 4, branches, params[0], moment[0], inputs[0], targets[0])


def solution(mesh):
    in_specs = (
        P("replica", "shard", None),
        P("replica", "shard", None),
        P("replica", "shard", None),
        P("replica", "shard", None),
        P(),
    )
    out_specs = (P("replica", "shard", None), P("replica", "shard", None))
    return jax.shard_map(local, mesh=mesh, in_specs=in_specs, out_specs=out_specs, check_vma=False)
```

```python
import jax
import jax.numpy as jnp
from jax import lax
from jax.experimental.layout import Layout, with_layout_constraint
from jax.sharding import PartitionSpec as P

BF16 = jnp.bfloat16
F32 = jnp.float32

CORE = [(i, i ^ 1) for i in range(16)]
ACROSS = [(i, i ^ 2) for i in range(16)]
UP = [(i, (i + 4) % 16) for i in range(16)]
DOWN = [(i, (i - 4) % 16) for i in range(16)]
FAR = [(i, (i + 8) % 16) for i in range(16)]
PLACES = [(dy, dz) for dy in range(4) for dz in range(2)]


def by_rows(value):
    return with_layout_constraint(value, Layout(major_to_minor=(0, 1)))


def move(value, route):
    return by_rows(lax.ppermute(by_rows(value), "shard", route))


def tied(value, *earlier):
    return lax.optimization_barrier((value, *earlier))[0]


def from_peer(value, distance):
    size = lax.axis_size("replica")
    return lax.ppermute(value, "replica", [((i + distance) % size, i) for i in range(size)])


def dot(a, b, over_a, over_b):
    return lax.dot_general(a, b, (((over_a,), (over_b,)), ((), ())), preferred_element_type=F32)


def halves(value, axis, first):
    low, high = jnp.split(value, 2, axis)
    return jnp.where(first, low, high), jnp.where(first, high, low)


def joined(kept, got, axis, first):
    return jnp.concatenate([jnp.where(first, kept, got), jnp.where(first, got, kept)], axis)


def gathered(block):
    across = move(block, ACROSS)
    far = move(block, FAR)
    below = move(block, UP)
    above = move(block, DOWN)
    return {
        (0, 0): block,
        (0, 1): across,
        (2, 0): far,
        (3, 0): below,
        (1, 0): above,
        (3, 1): move(across, UP),
        (1, 1): move(across, DOWN),
        (2, 1): move(far, ACROSS),
    }


def summed(part):
    low = lambda value: by_rows(value.astype(BF16))
    wide = lambda value: value.astype(F32)
    to_far = move(low(part(2, 1)), ACROSS)
    to_below = move(low(part(3, 1)), DOWN)
    to_above = move(low(part(1, 1)), UP)
    below = move(low(part(3, 0)), DOWN)
    above = move(low(part(1, 0)), UP)
    far = move(low(part(2, 0) + wide(to_far)), FAR)
    across = move(low(part(0, 1) + wide(to_below) + wide(to_above)), ACROSS)
    return part(0, 0) + wide(below) + wide(above) + wide(far) + wide(across)


def local_grad(lows, blocks, targets, tokens_all):
    pred = jnp.zeros(targets.shape, F32)
    for place, low in lows.items():
        pred = pred + dot(blocks[place], low, 1, 0)
    resid = (pred - targets.astype(F32)).astype(BF16)
    total = summed(lambda dy, dz: dot(blocks[dy, dz], resid, 0, 0))
    return by_rows(total) / jnp.float32(tokens_all)


def from_peers(values, level):
    def at(distance):
        return lambda *sent: tuple(from_peer(value, distance) for value in sent)

    low = [value.astype(BF16) for value in values]
    level = tied(level, *low)
    got = lax.switch(level, [at(2**power) for power in range(4)], *low)
    return [value.astype(F32) for value in got]


def local(params, moment, inputs, targets, step):
    place = lax.axis_index("shard")
    width = 2 * params.shape[1]
    half = params.shape[2] // 2
    tokens_all = inputs.shape[1] * lax.axis_size("shard")
    first = (place & 1) == 0
    z, y = (place >> 1) & 1, place >> 2
    starts = [(((y + dy) & 3) * 2 + (z ^ dz)) * width for dy, dz in PLACES]
    levels = [(step[0] + offset) & 3 for offset in range(2)]
    params, moment, inputs, targets, first, starts, levels = lax.optimization_barrier(
        (params[0], moment[0], inputs[0], targets[0], first, starts, levels)
    )

    low_kept, low_sent = halves(params.astype(BF16), 1, first)
    targets_kept, targets_sent = halves(targets, 1, first)
    got = move(jnp.concatenate([low_sent, targets_sent], 0), CORE)
    low = joined(low_kept, got[: width // 2], 0, first)
    targets = jnp.concatenate([targets_kept, got[width // 2 :]], 0)
    lows = gathered(low)

    inputs = tied(inputs, low)
    tokens = jnp.concatenate([inputs, move(inputs, CORE)], 0)
    blocks = {
        where: lax.dynamic_slice_in_dim(tokens, start, width, 1, allow_negative_indices=False)
        for where, start in zip(PLACES, starts)
    }

    both = tied(jnp.concatenate([params, moment], 0).reshape(2, *params.shape), lows[0, 1])
    kept, sent = halves(both, 2, first)
    got = lax.ppermute(sent, "shard", CORE)
    weights = by_rows(joined(kept[0], got[0], 0, first))
    momentum = by_rows(joined(kept[1], got[1], 0, first))

    grad = local_grad(lows, blocks, targets, tokens_all)
    upd_moment = 0.9 * momentum + grad
    upd_params = weights - 0.5 * upd_moment
    peer_params, peer_moment = from_peers((upd_params, upd_moment), levels[0])
    weights = 0.5 * (upd_params + peer_params)
    momentum = 0.5 * (upd_moment + peer_moment)

    lows = gathered(by_rows(weights.astype(BF16)))
    grad = local_grad(lows, blocks, targets, tokens_all)
    upd_moment = 0.9 * momentum + grad
    upd_params = weights - 0.5 * upd_moment
    kept, sent = halves(jnp.stack([upd_params, upd_moment]), 1, first)
    got = lax.ppermute(sent, "shard", CORE)
    upd_params = joined(kept[0], got[0], 1, first)
    upd_moment = joined(kept[1], got[1], 1, first)
    peer_params, peer_moment = from_peers((upd_params, upd_moment), levels[1])
    weights = 0.5 * (upd_params + peer_params)
    momentum = 0.5 * (upd_moment + peer_moment)
    return weights[None], momentum[None]


def solution(mesh):
    in_specs = (
        P("replica", "shard", None),
        P("replica", "shard", None),
        P("replica", "shard", None),
        P("replica", "shard", None),
        P(),
    )
    out_specs = (P("replica", "shard", None), P("replica", "shard", None))
    return jax.shard_map(local, mesh=mesh, in_specs=in_specs, out_specs=out_specs, check_vma=False)
```

```python
import jax
import jax.numpy as jnp
from jax import lax
from jax.experimental import pallas as pl
from jax.experimental.layout import Layout, with_layout_constraint
from jax.experimental.pallas import tpu as pltpu
from jax.sharding import PartitionSpec as P

BF16 = jnp.bfloat16
F32 = jnp.float32

CORE = [(i, i ^ 1) for i in range(16)]
ACROSS = [(i, i ^ 2) for i in range(16)]
UP = [(i, (i + 4) % 16) for i in range(16)]
DOWN = [(i, (i - 4) % 16) for i in range(16)]
FAR = [(i, (i + 8) % 16) for i in range(16)]
EARLY = [(0, 0), (0, 1), (2, 0), (3, 0), (1, 0)]
LATE = [(3, 1), (1, 1), (2, 1)]
PLACES = EARLY + LATE


def by_rows(value):
    return with_layout_constraint(value, Layout(major_to_minor=(0, 1)))


def move(value, route):
    return by_rows(lax.ppermute(by_rows(value), "shard", route))


def tied(value, *earlier):
    return lax.optimization_barrier((value, *earlier))[0]


def from_peer(value, distance):
    size = lax.axis_size("replica")
    return lax.ppermute(value, "replica", [((i + distance) % size, i) for i in range(size)])


def dot(a, b, over_a, over_b):
    return lax.dot_general(a, b, (((over_a,), (over_b,)), ((), ())), preferred_element_type=F32)


def halves(value, axis, first):
    size = value.shape[axis] // 2
    low, high = jnp.where(first, 0, size), jnp.where(first, size, 0)
    part = lambda start: lax.dynamic_slice_in_dim(value, start, size, axis, allow_negative_indices=False)
    return part(low), part(high)


def joined(kept, got, axis, first):
    return jnp.concatenate([jnp.where(first, kept, got), jnp.where(first, got, kept)], axis)


def gathered(block, tokens):
    across = move(block, ACROSS)
    far = move(block, FAR)
    below = move(block, UP)
    above = move(block, DOWN)
    late = [move(across, UP), move(across, DOWN), move(far, ACROSS)]
    early, tokens = lax.optimization_barrier(([block, across, far, below, above], tokens))
    return jnp.concatenate(early, 0), jnp.concatenate(late, 0), tokens


def summed(part, resid):
    low = lambda value: by_rows(value.astype(BF16))
    wide = lambda value: value.astype(F32)
    relayed = [low(part(resid, *where)) for where in LATE]
    to_below, to_above, to_far, resid = lax.optimization_barrier((*relayed, resid))
    to_far = move(to_far, ACROSS)
    to_below = move(to_below, DOWN)
    to_above = move(to_above, UP)
    direct = [low(part(resid, 3, 0)), low(part(resid, 1, 0))]
    below, above, resid = lax.optimization_barrier((*direct, resid))
    below = move(below, DOWN)
    above = move(above, UP)
    far = move(low(part(resid, 2, 0) + wide(to_far)), FAR)
    across = move(low(part(resid, 0, 1) + wide(to_below) + wide(to_above)), ACROSS)
    return part(resid, 0, 0) + wide(below) + wide(above) + wide(far) + wide(across)


def arrange_kernel(place, mine, other, first, second, sems):
    rows = mine.shape[0]
    z, y = (place[0] >> 1) & 1, place[0] >> 2
    width = mine.shape[1] // len(PLACES)
    copies = []
    for j in range(len(PLACES)):
        out, at = (first, j) if j < len(EARLY) else (second, j - len(EARLY))
        dy, dz = PLACES[j]
        chip = ((y + dy) & 3) * 2 + (z ^ dz)
        source = pl.ds(pl.multiple_of(chip * width, width), width)
        for h, x in enumerate((mine, other)):
            target = out.at[pl.ds(h * rows, rows), pl.ds(at * width, width)]
            copies.append(pltpu.make_async_copy(x.at[:, source], target, sems.at[j, h]))
    for copy in copies:
        copy.start()
    for copy in copies:
        copy.wait()


def arranged(mine, other, place):
    rows, width = mine.shape[0], mine.shape[1] // len(PLACES)
    shape = lambda places: jax.ShapeDtypeStruct((2 * rows, len(places) * width), mine.dtype)
    return pl.pallas_call(
        arrange_kernel,
        out_shape=[shape(EARLY), shape(LATE)],
        in_specs=[pl.BlockSpec(memory_space=pltpu.SMEM)] + [pl.BlockSpec(memory_space=pltpu.HBM)] * 2,
        out_specs=[pl.BlockSpec(memory_space=pltpu.VMEM)] * 2,
        scratch_shapes=[pltpu.SemaphoreType.DMA((len(PLACES), 2))],
        compiler_params=pltpu.CompilerParams(vmem_limit_bytes=24 * 2**20),
        cost_estimate=pl.CostEstimate(flops=0, bytes_accessed=0, transcendentals=0),
    )(place, mine, other)


def local_grad(block, mine, other, place, targets, tokens_all):
    first, second = arranged(mine, other, place)
    early, late, first = gathered(block, first)
    pred = dot(first, early, 1, 0)
    resid = (pred + dot(second, late, 1, 0) - targets.astype(F32)).astype(BF16)
    blocks = jnp.split(first, len(EARLY), 1) + jnp.split(second, len(LATE), 1)
    blocks = dict(zip(PLACES, blocks))
    total = summed(lambda resid, dy, dz: dot(blocks[dy, dz], resid, 0, 0), resid)
    return by_rows(total) / jnp.float32(tokens_all)


def from_peers(values, level):
    both = jnp.stack([value.astype(BF16) for value in values])
    got = lax.switch(
        tied(level, both), [lambda sent, power=power: from_peer(sent, 2**power) for power in range(4)], both
    )
    return got[0].astype(F32), got[1].astype(F32)


def local(params, moment, inputs, targets, step):
    place = lax.axis_index("shard")
    width = 2 * params.shape[1]
    half = params.shape[2] // 2
    tokens_all = inputs.shape[1] * lax.axis_size("shard")
    first = (place & 1) == 0
    place = place.reshape(1)
    levels = [(step[0] + offset) & 3 for offset in range(2)]
    params, moment, inputs, targets, first, place, levels = lax.optimization_barrier(
        (params[0], moment[0], inputs[0], targets[0], first, place, levels)
    )

    low_kept, low_sent = halves(params.astype(BF16), 1, first)
    targets_kept, targets_sent = halves(targets, 1, first)
    got = move(jnp.concatenate([low_sent, targets_sent], 0), CORE)
    block = joined(low_kept, got[: width // 2], 0, first)
    targets = jnp.concatenate([targets_kept, got[width // 2 :]], 0)
    mine = tied(inputs, block)
    other = move(mine, CORE)
    params, moment, _ = lax.optimization_barrier((params, moment, other))
    kept, sent = halves(jnp.stack([params, moment]), 2, first)
    got = lax.ppermute(sent, "shard", CORE)
    got, targets = lax.optimization_barrier((got, targets))
    weights = by_rows(joined(kept[0], got[0], 0, first))
    momentum = by_rows(joined(kept[1], got[1], 0, first))

    grad = local_grad(block, mine, other, place, targets, tokens_all)
    upd_moment = 0.9 * momentum + grad
    upd_params = weights - 0.5 * upd_moment
    peer_params, peer_moment = from_peers((upd_params, upd_moment), levels[0])
    weights = 0.5 * (upd_params + peer_params)
    momentum = 0.5 * (upd_moment + peer_moment)

    block = by_rows(weights.astype(BF16))
    mine, other, block = lax.optimization_barrier((mine, other, block))
    grad = local_grad(block, mine, other, place, targets, tokens_all)
    upd_moment = 0.9 * momentum + grad
    upd_params = weights - 0.5 * upd_moment
    kept, sent = halves(jnp.stack([upd_params, upd_moment]), 1, first)
    got = lax.ppermute(sent, "shard", CORE)
    upd_params = joined(kept[0], got[0], 1, first)
    upd_moment = joined(kept[1], got[1], 1, first)
    peer_params, peer_moment = from_peers((upd_params, upd_moment), levels[1])
    weights = 0.5 * (upd_params + peer_params)
    momentum = 0.5 * (upd_moment + peer_moment)
    return weights[None], momentum[None]


def solution(mesh):
    in_specs = (
        P("replica", "shard", None),
        P("replica", "shard", None),
        P("replica", "shard", None),
        P("replica", "shard", None),
        P(),
    )
    out_specs = (P("replica", "shard", None), P("replica", "shard", None))
    return jax.shard_map(local, mesh=mesh, in_specs=in_specs, out_specs=out_specs, check_vma=False)
```

```python
import jax
import jax.numpy as jnp
from jax import lax
from jax.experimental import pallas as pl
from jax.experimental.layout import Layout, with_layout_constraint
from jax.experimental.pallas import tpu as pltpu
from jax.sharding import PartitionSpec as P

BF16 = jnp.bfloat16
F32 = jnp.float32

CORE = [(i, i ^ 1) for i in range(16)]
ACROSS = [(i, i ^ 2) for i in range(16)]
UP = [(i, (i + 4) % 16) for i in range(16)]
DOWN = [(i, (i - 4) % 16) for i in range(16)]
FAR = [(i, (i + 8) % 16) for i in range(16)]
EARLY = [(0, 0), (0, 1), (2, 0), (3, 0), (1, 0)]
LATE = [(3, 1), (1, 1), (2, 1)]
PLACES = EARLY + LATE


def by_rows(value):
    return with_layout_constraint(value, Layout(major_to_minor=(0, 1)))


def move(value, route):
    return by_rows(lax.ppermute(by_rows(value), "shard", route))


def tied(value, *earlier):
    return lax.optimization_barrier((value, *earlier))[0]


def from_peer(value, distance):
    size = lax.axis_size("replica")
    return lax.ppermute(value, "replica", [((i + distance) % size, i) for i in range(size)])


def dot(a, b, over_a, over_b):
    return lax.dot_general(a, b, (((over_a,), (over_b,)), ((), ())), preferred_element_type=F32)


def halves(value, axis, first):
    size = value.shape[axis] // 2
    low, high = jnp.where(first, 0, size), jnp.where(first, size, 0)
    part = lambda start: lax.dynamic_slice_in_dim(value, start, size, axis, allow_negative_indices=False)
    return part(low), part(high)


def joined(kept, got, axis, first):
    return jnp.concatenate([jnp.where(first, kept, got), jnp.where(first, got, kept)], axis)


def gathered(block, first, second, together):
    across = move(block, ACROSS)
    far = move(block, FAR)
    below = move(block, UP)
    above = move(block, DOWN)
    late = [move(across, UP), move(across, DOWN), move(far, ACROSS)]
    early, first = lax.optimization_barrier(([block, across, far, below, above], first))
    if together:
        early, late, first, second = lax.optimization_barrier((early, late, first, second))
    return jnp.concatenate(early, 0), jnp.concatenate(late, 0), first, second


def summed(part, resid):
    low = lambda value: by_rows(value.astype(BF16))
    wide = lambda value: value.astype(F32)
    relayed = [low(part(resid, *where)) for where in LATE]
    to_below, to_above, to_far, resid = lax.optimization_barrier((*relayed, resid))
    to_far = move(to_far, ACROSS)
    to_below = move(to_below, DOWN)
    to_above = move(to_above, UP)
    direct = [low(part(resid, 3, 0)), low(part(resid, 1, 0))]
    below, above, resid = lax.optimization_barrier((*direct, resid))
    below = move(below, DOWN)
    above = move(above, UP)
    far = move(low(part(resid, 2, 0) + wide(to_far)), FAR)
    across = move(low(part(resid, 0, 1) + wide(to_below) + wide(to_above)), ACROSS)
    return part(resid, 0, 0) + wide(below) + wide(above) + wide(far) + wide(across)


def arrange_kernel(place, mine, other, first, second, sems):
    rows = mine.shape[0]
    z, y = (place[0] >> 1) & 1, place[0] >> 2
    width = mine.shape[1] // len(PLACES)
    copies = []
    for j in range(len(PLACES)):
        out, at = (first, j) if j < len(EARLY) else (second, j - len(EARLY))
        dy, dz = PLACES[j]
        chip = ((y + dy) & 3) * 2 + (z ^ dz)
        source = pl.ds(pl.multiple_of(chip * width, width), width)
        for h, x in enumerate((mine, other)):
            target = out.at[pl.ds(h * rows, rows), pl.ds(at * width, width)]
            copies.append(pltpu.make_async_copy(x.at[:, source], target, sems.at[j, h]))
    for copy in copies:
        copy.start()
    for copy in copies:
        copy.wait()


def arranged(mine, other, place):
    rows, width = mine.shape[0], mine.shape[1] // len(PLACES)
    shape = lambda places: jax.ShapeDtypeStruct((2 * rows, len(places) * width), mine.dtype)
    return pl.pallas_call(
        arrange_kernel,
        out_shape=[shape(EARLY), shape(LATE)],
        in_specs=[pl.BlockSpec(memory_space=pltpu.SMEM)] + [pl.BlockSpec(memory_space=pltpu.HBM)] * 2,
        out_specs=[pl.BlockSpec(memory_space=pltpu.VMEM)] * 2,
        scratch_shapes=[pltpu.SemaphoreType.DMA((len(PLACES), 2))],
        compiler_params=pltpu.CompilerParams(vmem_limit_bytes=24 * 2**20),
        cost_estimate=pl.CostEstimate(flops=0, bytes_accessed=0, transcendentals=0),
    )(place, mine, other)


def local_grad(block, mine, other, place, targets, tokens_all, together):
    first, second = arranged(mine, other, place)
    early, late, first, second = gathered(block, first, second, together)
    pred = dot(first, early, 1, 0)
    resid = (pred + dot(second, late, 1, 0) - targets.astype(F32)).astype(BF16)
    blocks = jnp.split(first, len(EARLY), 1) + jnp.split(second, len(LATE), 1)
    blocks = dict(zip(PLACES, blocks))
    total = summed(lambda resid, dy, dz: dot(blocks[dy, dz], resid, 0, 0), resid)
    return by_rows(total) / jnp.float32(tokens_all)


def from_peers(values, level):
    def at(distance):
        return lambda *sent: tuple(from_peer(value, distance) for value in sent)

    low = [value.astype(BF16) for value in values]
    got = lax.switch(tied(level, *low), [at(2**power) for power in range(4)], *low)
    return [value.astype(F32) for value in got]


def local(params, moment, inputs, targets, step):
    place = lax.axis_index("shard")
    width = 2 * params.shape[1]
    half = params.shape[2] // 2
    tokens_all = inputs.shape[1] * lax.axis_size("shard")
    first = (place & 1) == 0
    place = place.reshape(1)
    levels = [(step[0] + offset) & 3 for offset in range(2)]
    params, moment, inputs, targets, first, place, levels = lax.optimization_barrier(
        (params[0], moment[0], inputs[0], targets[0], first, place, levels)
    )

    low_kept, low_sent = halves(params.astype(BF16), 1, first)
    targets_kept, targets_sent = halves(targets, 1, first)
    got = move(jnp.concatenate([low_sent, targets_sent], 0), CORE)
    block = joined(low_kept, got[: width // 2], 0, first)
    targets = jnp.concatenate([targets_kept, got[width // 2 :]], 0)
    mine = tied(inputs, block)
    other = move(mine, CORE)
    params, moment, _ = lax.optimization_barrier((params, moment, other))
    kept, sent = halves(jnp.stack([params, moment]), 2, first)
    got = lax.ppermute(sent, "shard", CORE)
    got, targets = lax.optimization_barrier((got, targets))
    weights = by_rows(joined(kept[0], got[0], 0, first))
    momentum = by_rows(joined(kept[1], got[1], 0, first))

    grad = local_grad(block, mine, other, place, targets, tokens_all, False)
    upd_moment = 0.9 * momentum + grad
    upd_params = weights - 0.5 * upd_moment
    peer_params, peer_moment = from_peers((upd_params, upd_moment), levels[0])
    weights = 0.5 * (upd_params + peer_params)
    momentum = 0.5 * (upd_moment + peer_moment)

    block = by_rows(weights.astype(BF16))
    mine, other, block = lax.optimization_barrier((mine, other, block))
    grad = local_grad(block, mine, other, place, targets, tokens_all, True)
    upd_moment = 0.9 * momentum + grad
    upd_params = weights - 0.5 * upd_moment
    peer_params, peer_moment = from_peers((upd_params, upd_moment), levels[1])
    weights = 0.5 * (upd_params + peer_params)
    momentum = 0.5 * (upd_moment + peer_moment)
    kept, sent = halves(jnp.stack([weights, momentum]), 1, first)
    got = lax.ppermute(sent, "shard", CORE)
    weights = joined(kept[0], got[0], 1, first)
    momentum = joined(kept[1], got[1], 1, first)
    return weights[None], momentum[None]


def solution(mesh):
    in_specs = (
        P("replica", "shard", None),
        P("replica", "shard", None),
        P("replica", "shard", None),
        P("replica", "shard", None),
        P(),
    )
    out_specs = (P("replica", "shard", None), P("replica", "shard", None))
    return jax.shard_map(local, mesh=mesh, in_specs=in_specs, out_specs=out_specs, check_vma=False)
```

```python
import jax
import jax.numpy as jnp
from jax import lax
from jax.experimental import pallas as pl
from jax.experimental.layout import Layout, with_layout_constraint
from jax.experimental.pallas import tpu as pltpu
from jax.sharding import PartitionSpec as P

BF16 = jnp.bfloat16
F32 = jnp.float32

CORE = [(i, i ^ 1) for i in range(16)]
ACROSS = [(i, i ^ 2) for i in range(16)]
UP = [(i, (i + 4) % 16) for i in range(16)]
DOWN = [(i, (i - 4) % 16) for i in range(16)]
FAR = [(i, (i + 8) % 16) for i in range(16)]
EARLY = [(0, 0), (0, 1), (2, 0), (3, 0), (1, 0)]
LATE = [(3, 1), (1, 1), (2, 1)]
PLACES = EARLY + LATE


def by_rows(value):
    return with_layout_constraint(value, Layout(major_to_minor=(0, 1)))


def move(value, route):
    return by_rows(lax.ppermute(by_rows(value), "shard", route))


def tied(value, *earlier):
    return lax.optimization_barrier((value, *earlier))[0]


def from_peer(value, distance):
    size = lax.axis_size("replica")
    return lax.ppermute(value, "replica", [((i + distance) % size, i) for i in range(size)])


def dot(a, b, over_a, over_b):
    return lax.dot_general(a, b, (((over_a,), (over_b,)), ((), ())), preferred_element_type=F32)


def halves(value, axis, first):
    size = value.shape[axis] // 2
    low, high = jnp.where(first, 0, size), jnp.where(first, size, 0)
    part = lambda start: lax.dynamic_slice_in_dim(value, start, size, axis, allow_negative_indices=False)
    return part(low), part(high)


def joined(kept, got, axis, first):
    return jnp.concatenate([jnp.where(first, kept, got), jnp.where(first, got, kept)], axis)


def gathered(block, first, second, together):
    across = move(block, ACROSS)
    far = move(block, FAR)
    below = move(block, UP)
    above = move(block, DOWN)
    late = [move(across, UP), move(across, DOWN), move(far, ACROSS)]
    early, first = lax.optimization_barrier(([block, across, far, below, above], first))
    if together:
        early, late, first, second = lax.optimization_barrier((early, late, first, second))
    return jnp.concatenate(early, 0), jnp.concatenate(late, 0), first, second


def summed(part, resid):
    low = lambda value: by_rows(value.astype(BF16))
    wide = lambda value: value.astype(F32)
    relayed = [low(part(resid, *where)) for where in LATE]
    to_below, to_above, to_far, resid = lax.optimization_barrier((*relayed, resid))
    to_below = move(to_below, DOWN)
    to_above = move(to_above, UP)
    to_far = move(to_far, ACROSS)
    direct = [low(part(resid, 3, 0)), low(part(resid, 1, 0))]
    below, above, resid = lax.optimization_barrier((*direct, resid))
    below = move(below, DOWN)
    above = move(above, UP)
    far = move(low(part(resid, 2, 0) + wide(to_far)), FAR)
    across = move(low(part(resid, 0, 1) + wide(to_below) + wide(to_above)), ACROSS)
    return part(resid, 0, 0) + wide(below) + wide(above) + wide(far) + wide(across)


def arrange_kernel(place, mine, other, first, second, sems):
    rows = mine.shape[0]
    z, y = (place[0] >> 1) & 1, place[0] >> 2
    width = mine.shape[1] // len(PLACES)
    copies = []
    for j in range(len(PLACES)):
        out, at = (first, j) if j < len(EARLY) else (second, j - len(EARLY))
        dy, dz = PLACES[j]
        chip = ((y + dy) & 3) * 2 + (z ^ dz)
        source = pl.ds(pl.multiple_of(chip * width, width), width)
        for h, x in enumerate((mine, other)):
            target = out.at[pl.ds(h * rows, rows), pl.ds(at * width, width)]
            copies.append(pltpu.make_async_copy(x.at[:, source], target, sems.at[j, h]))
    for copy in copies:
        copy.start()
    for copy in copies:
        copy.wait()


def arranged(mine, other, place):
    rows, width = mine.shape[0], mine.shape[1] // len(PLACES)
    shape = lambda places: jax.ShapeDtypeStruct((2 * rows, len(places) * width), mine.dtype)
    return pl.pallas_call(
        arrange_kernel,
        out_shape=[shape(EARLY), shape(LATE)],
        in_specs=[pl.BlockSpec(memory_space=pltpu.SMEM)] + [pl.BlockSpec(memory_space=pltpu.HBM)] * 2,
        out_specs=[pl.BlockSpec(memory_space=pltpu.VMEM)] * 2,
        scratch_shapes=[pltpu.SemaphoreType.DMA((len(PLACES), 2))],
        compiler_params=pltpu.CompilerParams(vmem_limit_bytes=24 * 2**20),
        cost_estimate=pl.CostEstimate(flops=0, bytes_accessed=0, transcendentals=0),
    )(place, mine, other)


def local_grad(block, mine, other, place, targets, tokens_all, together):
    first, second = arranged(mine, other, place)
    early, late, first, second = gathered(block, first, second, together)
    pred = dot(first, early, 1, 0)
    resid = (pred + dot(second, late, 1, 0) - targets.astype(F32)).astype(BF16)
    blocks = jnp.split(first, len(EARLY), 1) + jnp.split(second, len(LATE), 1)
    blocks = dict(zip(PLACES, blocks))
    total = summed(lambda resid, dy, dz: dot(blocks[dy, dz], resid, 0, 0), resid)
    return by_rows(total) / jnp.float32(tokens_all)


def from_peers(values, level):
    def at(distance):
        return lambda *sent: tuple(from_peer(value, distance) for value in sent)

    low = [value.astype(BF16) for value in values]
    got = lax.switch(tied(level, *low), [at(2**power) for power in range(4)], *low)
    return [value.astype(F32) for value in got]


def local(params, moment, inputs, targets, step):
    place = lax.axis_index("shard")
    width = 2 * params.shape[1]
    half = params.shape[2] // 2
    tokens_all = inputs.shape[1] * lax.axis_size("shard")
    first = (place & 1) == 0
    place = place.reshape(1)
    levels = [(step[0] + offset) & 3 for offset in range(2)]
    params, moment, inputs, targets, first, place, levels = lax.optimization_barrier(
        (params[0], moment[0], inputs[0], targets[0], first, place, levels)
    )

    low_kept, low_sent = halves(params.astype(BF16), 1, first)
    block = joined(low_kept, move(low_sent, CORE), 0, first)
    mine = tied(inputs, block)
    other = move(mine, CORE)
    params, moment, targets, _ = lax.optimization_barrier((params, moment, targets, other))
    targets_kept, targets_sent = halves(targets, 1, first)
    targets = jnp.concatenate([targets_kept, move(targets_sent, CORE)], 0)
    kept, sent = halves(jnp.stack([params, moment]), 2, first)
    got = lax.ppermute(sent, "shard", CORE)
    got, targets = lax.optimization_barrier((got, targets))
    weights = by_rows(joined(kept[0], got[0], 0, first))
    momentum = by_rows(joined(kept[1], got[1], 0, first))

    grad = local_grad(block, mine, other, place, targets, tokens_all, False)
    upd_moment = 0.9 * momentum + grad
    upd_params = weights - 0.5 * upd_moment
    peer_params, peer_moment = from_peers((upd_params, upd_moment), levels[0])
    weights = 0.5 * (upd_params + peer_params)
    momentum = 0.5 * (upd_moment + peer_moment)

    block = by_rows(weights.astype(BF16))
    mine, other, block = lax.optimization_barrier((mine, other, block))
    grad = local_grad(block, mine, other, place, targets, tokens_all, True)
    upd_moment = 0.9 * momentum + grad
    upd_params = weights - 0.5 * upd_moment
    peer_params, peer_moment = from_peers((upd_params, upd_moment), levels[1])
    weights = 0.5 * (upd_params + peer_params)
    momentum = 0.5 * (upd_moment + peer_moment)
    kept, sent = halves(jnp.stack([weights, momentum]), 1, first)
    got = lax.ppermute(sent, "shard", CORE)
    weights = joined(kept[0], got[0], 1, first)
    momentum = joined(kept[1], got[1], 1, first)
    return weights[None], momentum[None]


def solution(mesh):
    in_specs = (
        P("replica", "shard", None),
        P("replica", "shard", None),
        P("replica", "shard", None),
        P("replica", "shard", None),
        P(),
    )
    out_specs = (P("replica", "shard", None), P("replica", "shard", None))
    return jax.shard_map(local, mesh=mesh, in_specs=in_specs, out_specs=out_specs, check_vma=False)
```

```python
import jax
import jax.numpy as jnp
from jax import lax
from jax.experimental import pallas as pl
from jax.experimental.layout import Layout, with_layout_constraint
from jax.experimental.pallas import tpu as pltpu
from jax.sharding import PartitionSpec as P

BF16 = jnp.bfloat16
F32 = jnp.float32

CORE = [(i, i ^ 1) for i in range(16)]
ACROSS = [(i, i ^ 2) for i in range(16)]
UP = [(i, (i + 4) % 16) for i in range(16)]
DOWN = [(i, (i - 4) % 16) for i in range(16)]
FAR = [(i, (i + 8) % 16) for i in range(16)]
EARLY = [(0, 0), (0, 1), (2, 0), (3, 0), (1, 0)]
LATE = [(3, 1), (1, 1), (2, 1)]
PLACES = EARLY + LATE


def by_rows(value):
    return with_layout_constraint(value, Layout(major_to_minor=(0, 1)))


def move(value, route):
    return by_rows(lax.ppermute(by_rows(value), "shard", route))


def tied(value, *earlier):
    return lax.optimization_barrier((value, *earlier))[0]


def from_peer(value, distance):
    size = lax.axis_size("replica")
    return lax.ppermute(value, "replica", [((i + distance) % size, i) for i in range(size)])


def dot(a, b, over_a, over_b):
    return lax.dot_general(a, b, (((over_a,), (over_b,)), ((), ())), preferred_element_type=F32)


def halves(value, axis, first):
    size = value.shape[axis] // 2
    low, high = jnp.where(first, 0, size), jnp.where(first, size, 0)
    part = lambda start: lax.dynamic_slice_in_dim(value, start, size, axis, allow_negative_indices=False)
    return part(low), part(high)


def joined(kept, got, axis, first):
    return jnp.concatenate([jnp.where(first, kept, got), jnp.where(first, got, kept)], axis)


def gathered(block, first, second, together):
    across = move(block, ACROSS)
    far = move(block, FAR)
    below = move(block, UP)
    above = move(block, DOWN)
    late = [move(across, UP), move(across, DOWN), move(far, ACROSS)]
    early, first = lax.optimization_barrier(([block, across, far, below, above], first))
    if together:
        early, late, first, second = lax.optimization_barrier((early, late, first, second))
    return jnp.concatenate(early, 0), jnp.concatenate(late, 0), first, second


def summed(part, resid):
    low = lambda value: by_rows(value.astype(BF16))
    wide = lambda value: value.astype(F32)
    relayed = [low(part(resid, *where)) for where in LATE]
    to_below, to_above, to_far, resid = lax.optimization_barrier((*relayed, resid))
    to_below = move(to_below, DOWN)
    to_above = move(to_above, UP)
    to_far = move(to_far, ACROSS)
    direct = [low(part(resid, 3, 0)), low(part(resid, 1, 0))]
    below, above, resid = lax.optimization_barrier((*direct, resid))
    below = move(below, DOWN)
    above = move(above, UP)
    far = move(low(part(resid, 2, 0) + wide(to_far)), FAR)
    across = move(low(part(resid, 0, 1) + wide(to_below) + wide(to_above)), ACROSS)
    return part(resid, 0, 0) + wide(below) + wide(above) + wide(far) + wide(across)


def arrange_kernel(place, mine, other, first, second, sems):
    rows = mine.shape[0]
    z, y = (place[0] >> 1) & 1, place[0] >> 2
    width = mine.shape[1] // len(PLACES)
    copies = []
    for j in range(len(PLACES)):
        out, at = (first, j) if j < len(EARLY) else (second, j - len(EARLY))
        dy, dz = PLACES[j]
        chip = ((y + dy) & 3) * 2 + (z ^ dz)
        source = pl.ds(pl.multiple_of(chip * width, width), width)
        for h, x in enumerate((mine, other)):
            target = out.at[pl.ds(h * rows, rows), pl.ds(at * width, width)]
            copies.append(pltpu.make_async_copy(x.at[:, source], target, sems.at[j, h]))
    for copy in copies:
        copy.start()
    for copy in copies:
        copy.wait()


def arranged(mine, other, place):
    rows, width = mine.shape[0], mine.shape[1] // len(PLACES)
    shape = lambda places: jax.ShapeDtypeStruct((2 * rows, len(places) * width), mine.dtype)
    return pl.pallas_call(
        arrange_kernel,
        out_shape=[shape(EARLY), shape(LATE)],
        in_specs=[pl.BlockSpec(memory_space=pltpu.SMEM)] + [pl.BlockSpec(memory_space=pltpu.HBM)] * 2,
        out_specs=[pl.BlockSpec(memory_space=pltpu.VMEM)] * 2,
        scratch_shapes=[pltpu.SemaphoreType.DMA((len(PLACES), 2))],
        compiler_params=pltpu.CompilerParams(vmem_limit_bytes=24 * 2**20),
        cost_estimate=pl.CostEstimate(flops=0, bytes_accessed=0, transcendentals=0),
    )(place, mine, other)


def local_grad(block, mine, other, place, targets, tokens_all, together):
    first, second = arranged(mine, other, place)
    early, late, first, second = gathered(block, first, second, together)
    pred = dot(first, early, 1, 0)
    resid = (pred + dot(second, late, 1, 0) - targets.astype(F32)).astype(BF16)
    blocks = jnp.split(first, len(EARLY), 1) + jnp.split(second, len(LATE), 1)
    blocks = dict(zip(PLACES, blocks))
    total = summed(lambda resid, dy, dz: dot(blocks[dy, dz], resid, 0, 0), resid)
    return by_rows(total) / jnp.float32(tokens_all)


def from_peers(values, level):
    def at(distance):
        return lambda *sent: tuple(from_peer(value, distance) for value in sent)

    low = [value.astype(BF16) for value in values]
    got = lax.switch(tied(level, *low), [at(2**power) for power in range(4)], *low)
    return [value.astype(F32) for value in got]


def local(params, moment, inputs, targets, step):
    place = lax.axis_index("shard")
    width = 2 * params.shape[1]
    half = params.shape[2] // 2
    tokens_all = inputs.shape[1] * lax.axis_size("shard")
    first = (place & 1) == 0
    place = place.reshape(1)
    levels = [(step[0] + offset) & 3 for offset in range(2)]
    params, moment, inputs, targets, first, place, levels = lax.optimization_barrier(
        (params[0], moment[0], inputs[0], targets[0], first, place, levels)
    )

    low_kept, low_sent = halves(params.astype(BF16), 1, first)
    block = joined(low_kept, move(low_sent, CORE), 0, first)
    mine = tied(inputs, block)
    other = move(mine, CORE)
    params, moment, targets, _ = lax.optimization_barrier((params, moment, targets, other))
    kept, sent = halves(jnp.concatenate([params, moment, targets.astype(F32)], 0), 1, first)
    got = lax.ppermute(sent, "shard", CORE)
    rows = params.shape[0]
    weights = by_rows(joined(kept[:rows], got[:rows], 0, first))
    momentum = by_rows(joined(kept[rows : 2 * rows], got[rows : 2 * rows], 0, first))
    targets = jnp.concatenate([kept[2 * rows :], got[2 * rows :]], 0)

    grad = local_grad(block, mine, other, place, targets, tokens_all, False)
    upd_moment = 0.9 * momentum + grad
    upd_params = weights - 0.5 * upd_moment
    peer_params, peer_moment = from_peers((upd_params, upd_moment), levels[0])
    weights = 0.5 * (upd_params + peer_params)
    momentum = 0.5 * (upd_moment + peer_moment)

    block = by_rows(weights.astype(BF16))
    mine, other, block = lax.optimization_barrier((mine, other, block))
    grad = local_grad(block, mine, other, place, targets, tokens_all, True)
    upd_moment = 0.9 * momentum + grad
    upd_params = weights - 0.5 * upd_moment
    peer_params, peer_moment = from_peers((upd_params, upd_moment), levels[1])
    weights = 0.5 * (upd_params + peer_params)
    momentum = 0.5 * (upd_moment + peer_moment)
    kept, sent = halves(jnp.stack([weights, momentum]), 1, first)
    got = lax.ppermute(sent, "shard", CORE)
    weights = joined(kept[0], got[0], 1, first)
    momentum = joined(kept[1], got[1], 1, first)
    return weights[None], momentum[None]


def solution(mesh):
    in_specs = (
        P("replica", "shard", None),
        P("replica", "shard", None),
        P("replica", "shard", None),
        P("replica", "shard", None),
        P(),
    )
    out_specs = (P("replica", "shard", None), P("replica", "shard", None))
    return jax.shard_map(local, mesh=mesh, in_specs=in_specs, out_specs=out_specs, check_vma=False)
```
